32 devices in a mesh: groups: 2 (over x), row: 16 (over z, y, core).
Axes of the slice: x: 2, y: 2, z: 4, core: 2. Of those that a mesh axis runs over, the one named last changes fastest.
Arguments:
- pair: bfloat16 [512, 256, 128], P(('groups', 'row')), parts along dimension 0, may hold values from -6 to 6
- residue_mask: int32 [512], P('groups'), parts along dimension 0, may hold values 0 or 1
- ln_in_gain: float32 [128], replicated, may hold values from 0.1 to 1.9
- w_a_gate: bfloat16 [128, 128], replicated, may hold values from -0.5 to 0.5
- w_a_proj: bfloat16 [128, 128], replicated, may hold values from -0.5 to 0.5
- w_b_gate: bfloat16 [128, 128], replicated, may hold values from -0.5 to 0.5
- w_b_proj: bfloat16 [128, 128], replicated, may hold values from -0.5 to 0.5
- w_out_gate: bfloat16 [128, 128], replicated, may hold values from -0.5 to 0.5
- ln_out_gain: float32 [128], replicated, may hold values from 0.1 to 1.9
- w_out: bfloat16 [128, 128], replicated, may hold values from -0.5 to 0.5
Outputs:
- pair_columns: bfloat16 [512, 256, 128], P('groups', 'row'), parts along dimension 0
The draws below stay inside these ranges and needn't reach their ends.
There are 2 independent parts, one for each index of `groups`. The reference program is written for one: setup_inputs(seed, part) draws one part's arguments, and reference() takes and returns one part's arrays. A program takes and returns all parts, laid end to end along the dimension named above; an argument that names none is the same for every part. Nothing has to cross between parts.
Inputs may be any that keep to these rules, and one draw needn't show every extreme that they name: `residue_mask`: 256 flags, 1 for a resolved token.
All inputs are finite; a program needn't handle non-finite values.
Results may differ from the reference program's by a relative error of at most 0.002.
Values may be sent and summed in bfloat16 or wider, within the bound.
A program may use at most 128 MiB of HBM per device.

```python
import jax
import jax.numpy as jnp
from jax import lax

CH = 128
TOK_DEV = 16
TOKENS = 256
N_ROW = 16


def plant(entries, stream_key, smallest, high):
    dims = entries.shape
    index_at = [jax.random.randint(jax.random.fold_in(stream_key, axis), (), 0, dims[axis]) for axis in range(len(dims))]
    entries = entries.at[tuple(index_at)].set(smallest)
    longest = dims.index(max(dims))
    index_at[longest] = (index_at[longest] + 1) % dims[longest]
    return entries.at[tuple(index_at)].set(high)


def levels(rng, dims, cuts, low, largest):
    def one(axis_at, shards_of):
        draws = jax.random.uniform(jax.random.fold_in(jax.random.fold_in(rng, 6), axis_at), (shards_of,), jnp.float32, low / len(cuts), largest / len(cuts))
        return jnp.repeat(jnp.exp(draws), dims[axis_at] // shards_of).reshape((-1,) + (1,) * (len(dims) - axis_at - 1))

    gain = one(*cuts[0])
    for cut in cuts[1:]:
        gain = gain * one(*cut)
    return gain


def normal_values(rng, dims, deviation, limit, pieces=(), kind=jnp.bfloat16):
    level = levels(rng, dims, pieces, -0.22, 0.18) if pieces else 1.0
    values = jax.random.normal(rng, dims, jnp.float32) * deviation * level
    return jnp.minimum(jnp.maximum(values, -limit), limit).astype(kind)


def setup_inputs(seed: int = 0, part: int = 0) -> dict:
    key_of = jax.random.split(jax.random.key(seed), 11)
    part_splits = jax.random.split(jax.random.fold_in(key_of[10], part), 11)
    pair = normal_values(part_splits[0], (TOKENS, TOKENS, CH), 1.0, 6.0, ((0, 16),))
    residue_mask = plant((jax.random.randint(part_splits[1], (TOKENS,), 0, 4) < 3).astype(jnp.int32), jax.random.fold_in(part_splits[1], 1), 0, 1)
    ln_in_gain = jnp.clip(1.0 + 0.18 * jax.random.normal(key_of[2], (CH,), jnp.float32), 0.1, 1.9)
    w_a_gate = normal_values(key_of[3], (CH, CH), CH ** -0.5, 0.5)
    w_a_proj = normal_values(key_of[4], (CH, CH), CH ** -0.5, 0.5)
    w_b_gate = normal_values(key_of[5], (CH, CH), CH ** -0.5, 0.5)
    w_b_proj = normal_values(key_of[6], (CH, CH), CH ** -0.5, 0.5)
    w_out_gate = normal_values(key_of[7], (CH, CH), CH ** -0.5, 0.5)
    ln_out_gain = jnp.clip(1.0 + 0.18 * jax.random.normal(key_of[8], (CH,), jnp.float32), 0.1, 1.9)
    w_out = normal_values(key_of[9], (CH, CH), CH ** -0.5, 0.5)
    return {"pair": pair, "residue_mask": residue_mask, "ln_in_gain": ln_in_gain, "w_a_gate": w_a_gate, "w_a_proj": w_a_proj, "w_b_gate": w_b_gate, "w_b_proj": w_b_proj, "w_out_gate": w_out_gate, "ln_out_gain": ln_out_gain, "w_out": w_out}


epsilon = 1e-05

def normalize(values, scale_gain):
    center = lax.optimization_barrier(jnp.mean(values, axis=-1, keepdims=True))
    centered = values - center
    spread = lax.optimization_barrier(jnp.mean(centered * centered, axis=-1, keepdims=True))
    return centered * lax.rsqrt(spread + epsilon) * scale_gain

def gated_proj(flat_rows, weight_gate, weight_proj):
    gating = jnp.dot(flat_rows, weight_gate, preferred_element_type=jnp.float32)
    projected = jnp.dot(flat_rows, weight_proj, preferred_element_type=jnp.float32)
    return jax.nn.sigmoid(gating) * projected

def reference(pair, residue_mask, ln_in_gain, w_a_gate, w_a_proj, w_b_gate, w_b_proj, w_out_gate, ln_out_gain, w_out):
    mask_float = residue_mask.astype(jnp.float32)
    pair_blocks = pair.reshape(N_ROW, TOK_DEV, TOKENS, CH)
    mask_blocks = mask_float.reshape(N_ROW, TOK_DEV)

    def normed_rows(row_part):
        return normalize(row_part.astype(jnp.float32), ln_in_gain).astype(jnp.bfloat16)

    def make_right(operands):
        row_part, row_mask = operands
        normed = normed_rows(row_part).reshape(TOK_DEV * TOKENS, CH)
        values = gated_proj(normed, w_b_gate, w_b_proj).reshape(TOK_DEV, TOKENS, CH)
        values = values * row_mask[:, None, None] * mask_float[None, :, None]
        return values.astype(jnp.bfloat16)
    right_all = lax.map(make_right, (pair_blocks, mask_blocks))

    def update_block(operands):
        row_part, row_mask, position = operands
        normed = normed_rows(row_part)
        left = gated_proj(normed.reshape(TOK_DEV * TOKENS, CH), w_a_gate, w_a_proj).reshape(TOK_DEV, TOKENS, CH)
        left = (left * row_mask[:, None, None] * mask_float[None, :, None]).astype(jnp.bfloat16)
        result = row_part
        for offset in range(3):
            column_block = ((position - offset) % N_ROW).astype(jnp.int32)
            right = lax.dynamic_index_in_dim(right_all, column_block, 0, keepdims=False)
            product = jnp.einsum('ikc,jkc->ijc', left.astype(jnp.float32), right.astype(jnp.float32))
            normed_x = normalize(product, ln_out_gain).astype(jnp.bfloat16).reshape(TOK_DEV * TOK_DEV, CH)
            update = jnp.dot(normed_x, w_out, preferred_element_type=jnp.float32)
            start = (column_block * TOK_DEV).astype(jnp.int32)
            columns = lax.dynamic_slice_in_dim(normed, start, TOK_DEV, 1).reshape(TOK_DEV * TOK_DEV, CH)
            gating = jax.nn.sigmoid(jnp.dot(columns, w_out_gate, preferred_element_type=jnp.float32))
            old_block = lax.dynamic_slice_in_dim(row_part, start, TOK_DEV, 1)
            new_block = (old_block.astype(jnp.float32) + (gating * update).reshape(TOK_DEV, TOK_DEV, CH)).astype(jnp.bfloat16)
            result = lax.dynamic_update_slice_in_dim(result, new_block, start, 1)
        return result
    updated = lax.map(update_block, (pair_blocks, mask_blocks, jnp.arange(N_ROW, dtype=jnp.int32)))
    return updated.reshape(TOKENS, TOKENS, CH)
```

```python
import functools

import jax
import jax.numpy as jnp
from jax import lax
from jax.experimental import pallas as pl
from jax.experimental.pallas import tpu as pltpu
from jax.sharding import PartitionSpec as P

EPSILON = 1e-05
MESH = pl.DeviceIdType.MESH
CHUNKS = 4
STEPS = 4


def normalize(values, gain):
    center = jnp.mean(values, axis=-1, keepdims=True)
    centered = values - center
    spread = jnp.mean(centered * centered, axis=-1, keepdims=True)
    return centered * lax.rsqrt(spread + EPSILON) * gain


def dot(a, b):
    return jnp.dot(a, b, preferred_element_type=jnp.float32)


def kernel(
    blocks,
    pair,
    mask,
    in_gain,
    w_a_gate,
    w_a_proj,
    w_b_gate,
    w_b_proj,
    w_out_gate,
    out_gain,
    w_out,
    out,
    halo,
    left,
    right,
    product,
    token_mask,
    halo_send,
    halo_recv,
    forward_send,
    block_send,
    block_recv,
):
    rows, tokens, channels = pair.shape
    me = lax.axis_index("row")
    odd = lax.rem(me, 2)
    part = rows // CHUNKS
    own = pl.multiple_of(me * rows, rows)

    def at(distance):
        return {"row": lax.rem(me + distance + blocks, blocks)}

    barrier = pltpu.get_barrier_semaphore()

    def greet(distance, _):
        pl.semaphore_signal(barrier, inc=1, device_id=at(distance), device_id_type=MESH)
        return 0

    lax.fori_loop(1, blocks, greet, 0)
    pl.semaphore_wait(barrier, blocks - 1)

    def halo_copy(distance, chunk):
        slot = distance - 1
        piece = pl.ds(chunk * part, part)
        return pltpu.make_async_remote_copy(
            src_ref=pair.at[piece],
            dst_ref=halo.at[slot, piece],
            send_sem=halo_send.at[slot, chunk],
            recv_sem=halo_recv.at[slot, chunk],
            device_id=at(-distance),
            device_id_type=MESH,
        )

    half = CHUNKS // 2

    def halo_all(act):
        for chunk in range(half):
            act(halo_copy(2, chunk))
            pl.when(odd == 0)(lambda chunk=chunk: act(halo_copy(1, half + chunk)))
            pl.when(odd == 1)(lambda chunk=chunk: act(halo_copy(2, half + chunk)))
        for chunk in range(half):
            pl.when(odd == 1)(lambda chunk=chunk: act(halo_copy(1, chunk)))
            pl.when(odd == 1)(lambda chunk=chunk: act(halo_copy(1, half + chunk)))

    halo_all(lambda copy: copy.start())

    def block_copy(distance):
        target = lax.rem(me + distance, blocks)
        columns = pl.ds(pl.multiple_of(target * rows, rows), rows)
        return pltpu.make_async_remote_copy(
            src_ref=pair.at[:, columns],
            dst_ref=out.at[pl.ds(own, rows)],
            send_sem=block_send.at[distance],
            recv_sem=block_recv.at[distance],
            device_id={"row": target},
            device_id_type=MESH,
        )

    def send_block(distance, _):
        block_copy(distance).start()
        return 0

    lax.fori_loop(1, blocks - 2, send_block, 0)

    mask_row = mask[...].astype(jnp.float32)
    token_mask[...] = jnp.broadcast_to(mask_row, (channels, tokens)).T

    def make_right(i, _):
        normed = normalize(pair[i].astype(jnp.float32), in_gain[...]).astype(jnp.bfloat16)
        values = jax.nn.sigmoid(dot(normed, w_b_gate[...])) * dot(normed, w_b_proj[...])
        values = values * token_mask[...] * token_mask[pl.ds(own + i, 1), :]
        right[i] = values.astype(jnp.bfloat16).astype(jnp.float32)
        return 0

    lax.fori_loop(0, rows, make_right, 0)

    def process(read, owner):
        def make_left(i, _):
            normed = normalize(read(i).astype(jnp.float32), in_gain[...]).astype(jnp.bfloat16)
            values = jax.nn.sigmoid(dot(normed, w_a_gate[...])) * dot(normed, w_a_proj[...])
            left[i] = values.astype(jnp.bfloat16).astype(jnp.float32)
            return 0

        lax.fori_loop(0, rows, make_left, 0)
        first = pl.multiple_of(owner * rows, rows)

        def tile(t, _):
            i = (t // (rows // 8)) * 2
            j = pl.multiple_of((t % (rows // 8)) * 8, 8)

            def body(step, sums):
                sums = list(sums)
                for s in range(STEPS):
                    k = pl.ds(pl.multiple_of(step * (8 * STEPS) + s * 8, 8), 8)
                    ls = [left[i + a, k, :] for a in range(2)]
                    for b in range(8):
                        r = right[j + b, k, :]
                        for a in range(2):
                            sums[a * 8 + b] = sums[a * 8 + b] + ls[a] * r
                return tuple(sums)

            zero = jnp.zeros((8, channels), jnp.float32)
            sums = lax.fori_loop(0, tokens // (8 * STEPS), body, (zero,) * 16)
            for a in range(2):
                joined = jnp.concatenate(
                    [jnp.sum(sums[a * 8 + b], axis=0, keepdims=True) for b in range(8)], axis=0
                )
                product[i + a, pl.ds(j, 8), :] = joined * token_mask[pl.ds(first + i + a, 1), :]
            return 0

        lax.fori_loop(0, (rows // 2) * (rows // 8), tile, 0)
        normed_x = normalize(product[...], out_gain[...]).astype(jnp.bfloat16)
        update = dot(normed_x.reshape(rows * rows, channels), w_out[...])
        old = read(slice(None), pl.ds(own, rows)).astype(jnp.float32)
        normed = normalize(old, in_gain[...]).astype(jnp.bfloat16)
        gating = jax.nn.sigmoid(dot(normed.reshape(rows * rows, channels), w_out_gate[...]))
        new = old + (gating * update).reshape(rows, rows, channels)
        out[pl.ds(first, rows)] = new.astype(jnp.bfloat16)

    process(lambda *index: pair[index], me)

    def arrival(slot, chunk):
        piece = pl.ds(chunk * part, part)
        return pltpu.make_async_remote_copy(
            src_ref=pair.at[piece],
            dst_ref=halo.at[slot, piece],
            send_sem=halo_send.at[slot, chunk],
            recv_sem=halo_recv.at[slot, chunk],
            device_id=at(1 - 2 * odd),
            device_id_type=MESH,
        )

    def forward(c):
        chunk = odd * half + c
        piece = pl.ds(chunk * part, part)
        return pltpu.make_async_remote_copy(
            src_ref=halo.at[1 - odd, piece],
            dst_ref=halo.at[odd, piece],
            send_sem=forward_send.at[c],
            recv_sem=halo_recv.at[odd, chunk],
            device_id=at(1 - 2 * odd),
            device_id_type=MESH,
        )

    for c in range(half):
        arrival(1 - odd, odd * half + c).wait_recv()
        forward(c).start()

    def halo_step(step, _):
        slot = lax.rem(odd + step, 2)

        @pl.when(step == 0)
        def _():
            for chunk in range(CHUNKS):
                arrival(odd, chunk).wait_recv()

        @pl.when(step == 1)
        def _():
            for c in range(half):
                arrival(1 - odd, (1 - odd) * half + c).wait_recv()

        process(lambda *index: halo[(slot,) + index], lax.rem(me + 1 + slot, blocks))
        return 0

    lax.fori_loop(0, 2, halo_step, 0)

    for c in range(half):
        forward(c).wait_send()
    halo_all(lambda copy: copy.wait_send())

    def finish_block(distance, _):
        source = lax.rem(me - distance + blocks, blocks)
        columns = pl.ds(own, rows)
        landed = pltpu.make_async_remote_copy(
            src_ref=pair.at[:, columns],
            dst_ref=out.at[pl.ds(pl.multiple_of(source * rows, rows), rows)],
            send_sem=block_send.at[distance],
            recv_sem=block_recv.at[distance],
            device_id={"row": source},
            device_id_type=MESH,
        )
        landed.wait_recv()
        block_copy(distance).wait_send()
        return 0

    lax.fori_loop(1, blocks - 2, finish_block, 0)


def shards(blocks, pair, residue_mask, ln_in_gain, *rest):
    w_a_gate, w_a_proj, w_b_gate, w_b_proj, w_out_gate, ln_out_gain, w_out = rest
    rows, tokens, channels = pair.shape
    vmem = pl.BlockSpec(memory_space=pltpu.VMEM)
    return pl.pallas_call(
        functools.partial(kernel, blocks),
        out_shape=jax.ShapeDtypeStruct((tokens, rows, channels), jnp.bfloat16),
        in_specs=[vmem] * 10,
        out_specs=vmem,
        scratch_shapes=[
            pltpu.VMEM((2, rows, tokens, channels), jnp.bfloat16),
            pltpu.VMEM((rows, tokens, channels), jnp.float32),
            pltpu.VMEM((rows, tokens, channels), jnp.float32),
            pltpu.VMEM((rows, rows, channels), jnp.float32),
            pltpu.VMEM((tokens, channels), jnp.float32),
            pltpu.SemaphoreType.DMA((2, CHUNKS)),
            pltpu.SemaphoreType.DMA((2, CHUNKS)),
            pltpu.SemaphoreType.DMA((CHUNKS // 2,)),
            pltpu.SemaphoreType.DMA((blocks,)),
            pltpu.SemaphoreType.DMA((blocks,)),
        ],
        compiler_params=pltpu.CompilerParams(
            collective_id=0, has_side_effects=True, vmem_limit_bytes=48 * 2**20
        ),
    )(
        pair,
        residue_mask.reshape(1, tokens),
        ln_in_gain.reshape(1, channels),
        w_a_gate,
        w_a_proj,
        w_b_gate,
        w_b_proj,
        w_out_gate,
        ln_out_gain.reshape(1, channels),
        w_out,
    )


def solution(mesh):
    placed = (P(("groups", "row"), None, None), P("groups"), P(), P(), P(), P(), P(), P(), P(), P())
    return jax.shard_map(
        functools.partial(shards, mesh.shape["row"]),
        mesh=mesh,
        in_specs=placed,
        out_specs=P("groups", "row", None),
        check_vma=False,
    )
```

```python
import functools

import jax
import jax.numpy as jnp
from jax import lax
from jax.experimental import pallas as pl
from jax.experimental.pallas import tpu as pltpu
from jax.sharding import PartitionSpec as P

EPSILON = 1e-05
MESH = pl.DeviceIdType.MESH
CHUNKS = 4
STEPS = 4
GROUP = 1024
LIMIT = 63 * 2**20


def normalize(values, gain):
    center = jnp.mean(values, axis=-1, keepdims=True)
    centered = values - center
    spread = jnp.mean(centered * centered, axis=-1, keepdims=True)
    return centered * lax.rsqrt(spread + EPSILON) * gain


def half_sigmoid(values):
    return 1.0 + jnp.tanh(0.5 * values)


def dot(a, b):
    return jnp.dot(a, b, preferred_element_type=jnp.float32)


def kernel(
    blocks,
    pair,
    mask_arg,
    in_gain_arg,
    w_a_gate,
    w_a_proj,
    w_b_gate,
    w_b_proj,
    w_out_gate_arg,
    out_gain_arg,
    w_out_arg,
    out,
    own_pair,
    mask,
    in_gain,
    w_in,
    w_out_gate,
    out_gain,
    w_out,
    load,
    halo,
    left,
    right,
    product,
    token_mask,
    halo_send,
    halo_recv,
    forward_send,
    block_send,
    block_recv,
):
    rows, tokens, channels = pair.shape
    me = lax.axis_index("row")
    odd = lax.rem(me, 2)
    part = rows // CHUNKS
    own = pl.multiple_of(me * rows, rows)

    def at(distance):
        return {"row": lax.rem(me + distance + blocks, blocks)}

    barrier = pltpu.get_barrier_semaphore()

    def greet(distance, _):
        pl.semaphore_signal(barrier, inc=1, device_id=at(distance), device_id_type=MESH)
        return 0

    lax.fori_loop(1, blocks, greet, 0)
    loads = [(pair, own_pair), (mask_arg, mask), (in_gain_arg, in_gain)]
    for n, w in enumerate((w_a_gate, w_a_proj, w_b_gate, w_b_proj)):
        loads.append((w, w_in.at[:, n * channels : (n + 1) * channels]))
    loads += [(w_out_gate_arg, w_out_gate), (out_gain_arg, out_gain), (w_out_arg, w_out)]
    loads = [pltpu.make_async_copy(a, b, load.at[n]) for n, (a, b) in enumerate(loads)]
    for copy in loads:
        copy.start()
    pl.semaphore_wait(barrier, blocks - 1)

    half = CHUNKS // 2

    def span(chunk):
        return pl.ds(chunk * part, part)

    def distance_of(chunk):
        return 1 + odd if chunk >= half else 2

    def direct(chunk):
        distance = distance_of(chunk)
        return pltpu.make_async_remote_copy(
            src_ref=pair.at[span(chunk)],
            dst_ref=halo.at[distance - 1, span(chunk)],
            send_sem=halo_send.at[0, chunk],
            recv_sem=halo_recv.at[distance - 1, chunk],
            device_id=at(-distance),
            device_id_type=MESH,
        )

    def inner(chunk):
        return pltpu.make_async_remote_copy(
            src_ref=pair.at[span(chunk)],
            dst_ref=halo.at[0, span(chunk)],
            send_sem=halo_send.at[1, chunk],
            recv_sem=halo_recv.at[0, chunk],
            device_id=at(-1),
            device_id_type=MESH,
        )

    def halo_all(act):
        for chunk in range(CHUNKS):
            act(direct(chunk))
        for chunk in range(CHUNKS):
            pl.when(odd == 1)(lambda chunk=chunk: act(inner(chunk)))

    halo_all(lambda copy: copy.start())

    def block_copy(distance):
        target = lax.rem(me + distance, blocks)
        columns = pl.ds(pl.multiple_of(target * rows, rows), rows)
        return pltpu.make_async_remote_copy(
            src_ref=pair.at[:, columns],
            dst_ref=out.at[pl.ds(own, rows)],
            send_sem=block_send.at[distance],
            recv_sem=block_recv.at[distance],
            device_id={"row": target},
            device_id_type=MESH,
        )

    def send_block(distance, _):
        block_copy(distance).start()
        return 0

    lax.fori_loop(1, blocks - 2, send_block, 0)

    for copy in loads:
        copy.wait()
    token_mask[...] = jnp.broadcast_to(mask[...].astype(jnp.float32), (channels, tokens)).T

    batch = max(1, GROUP // tokens)

    def normed_of(values):
        single = jnp.full((channels, channels), 1.0 / channels, jnp.bfloat16)
        double = jnp.full((2 * channels, channels), 1.0 / channels, jnp.bfloat16)
        centered = values.astype(jnp.float32) - dot(values, single)
        square = centered * centered
        high = square.astype(jnp.bfloat16)
        low = (square - high.astype(jnp.float32)).astype(jnp.bfloat16)
        spread = dot(jnp.concatenate([high, low], axis=1), double)
        return (centered * lax.rsqrt(spread + EPSILON) * in_gain[...]).astype(jnp.bfloat16)

    def gated(gates, values):
        return (0.5 * half_sigmoid(gates) * values).reshape(batch, tokens, channels)

    def project(read, with_right):
        def step(n, _):
            some = pl.ds(n * batch, batch)
            normed = normed_of(read(some).reshape(batch * tokens, channels))
            a = dot(normed, w_in[:, : 2 * channels])
            values = gated(a[:, :channels], a[:, channels:])
            left[some] = values.astype(jnp.bfloat16).astype(jnp.float32)
            if with_right:
                b = dot(normed, w_in[:, 2 * channels :])
                values = gated(b[:, :channels], b[:, channels:]) * token_mask[...]
                for i in range(batch):
                    row = values[i] * token_mask[pl.ds(own + n * batch + i, 1), :]
                    right[n * batch + i] = row.astype(jnp.bfloat16).astype(jnp.float32)
            return 0

        lax.fori_loop(0, rows // batch, step, 0)

    def process(read, owner):
        first = pl.multiple_of(owner * rows, rows)

        def tile(t, _):
            i = (t // (rows // 8)) * 2
            j = pl.multiple_of((t % (rows // 8)) * 8, 8)

            def body(step, sums):
                sums = list(sums)
                for s in range(STEPS):
                    k = pl.ds(pl.multiple_of(step * (8 * STEPS) + s * 8, 8), 8)
                    ls = [left[i + a, k, :] for a in range(2)]
                    for b in range(8):
                        r = right[j + b, k, :]
                        for a in range(2):
                            sums[a * 8 + b] = sums[a * 8 + b] + ls[a] * r
                return tuple(sums)

            zero = jnp.zeros((8, channels), jnp.float32)
            sums = lax.fori_loop(0, tokens // (8 * STEPS), body, (zero,) * 16)
            for a in range(2):
                joined = jnp.concatenate(
                    [jnp.sum(sums[a * 8 + b], axis=0, keepdims=True) for b in range(8)], axis=0
                )
                product[i + a, pl.ds(j, 8), :] = joined * token_mask[pl.ds(first + i + a, 1), :]
            return 0

        lax.fori_loop(0, (rows // 2) * (rows // 8), tile, 0)
        normed_x = normalize(product[...], out_gain[...]).astype(jnp.bfloat16)
        update = dot(normed_x.reshape(rows * rows, channels), w_out[...])
        old = read(slice(None), pl.ds(own, rows)).astype(jnp.float32)
        normed = normalize(old, in_gain[...]).astype(jnp.bfloat16)
        gating = jax.nn.sigmoid(dot(normed.reshape(rows * rows, channels), w_out_gate[...]))
        new = old + (gating * update).reshape(rows, rows, channels)
        out[pl.ds(first, rows)] = new.astype(jnp.bfloat16)

    def own_rows(*index):
        return own_pair[index]

    project(own_rows, True)

    process(own_rows, me)

    def arrival(slot, chunk):
        piece = pl.ds(chunk * part, part)
        return pltpu.make_async_remote_copy(
            src_ref=pair.at[piece],
            dst_ref=halo.at[slot, piece],
            send_sem=halo_send.at[slot, chunk],
            recv_sem=halo_recv.at[slot, chunk],
            device_id=at(1 - 2 * odd),
            device_id_type=MESH,
        )

    def forward(c):
        chunk = odd * half + c
        piece = pl.ds(chunk * part, part)
        return pltpu.make_async_remote_copy(
            src_ref=halo.at[1 - odd, piece],
            dst_ref=halo.at[odd, piece],
            send_sem=forward_send.at[c],
            recv_sem=halo_recv.at[odd, chunk],
            device_id=at(1 - 2 * odd),
            device_id_type=MESH,
        )

    for c in range(half):
        arrival(1 - odd, odd * half + c).wait_recv()
        forward(c).start()

    def halo_step(step, _):
        slot = lax.rem(odd + step, 2)

        @pl.when(step == 0)
        def _():
            for chunk in range(CHUNKS):
                arrival(odd, chunk).wait_recv()

        @pl.when(step == 1)
        def _():
            for c in range(half):
                arrival(1 - odd, (1 - odd) * half + c).wait_recv()

        def halo_rows(*index):
            return halo[(slot,) + index]

        project(halo_rows, False)
        process(halo_rows, lax.rem(me + 1 + slot, blocks))
        return 0

    lax.fori_loop(0, 2, halo_step, 0)

    for c in range(half):
        forward(c).wait_send()
    halo_all(lambda copy: copy.wait_send())

    def finish_block(distance, _):
        source = lax.rem(me - distance + blocks, blocks)
        columns = pl.ds(own, rows)
        landed = pltpu.make_async_remote_copy(
            src_ref=pair.at[:, columns],
            dst_ref=out.at[pl.ds(pl.multiple_of(source * rows, rows), rows)],
            send_sem=block_send.at[distance],
            recv_sem=block_recv.at[distance],
            device_id={"row": source},
            device_id_type=MESH,
        )
        landed.wait_recv()
        block_copy(distance).wait_send()
        return 0

    lax.fori_loop(1, blocks - 2, finish_block, 0)


def shards(blocks, pair, residue_mask, ln_in_gain, *rest):
    w_a_gate, w_a_proj, w_b_gate, w_b_proj, w_out_gate, ln_out_gain, w_out = rest
    rows, tokens, channels = pair.shape
    weight = pltpu.VMEM((channels, channels), jnp.bfloat16)
    gain = pltpu.VMEM((1, channels), jnp.float32)
    return pl.pallas_call(
        functools.partial(kernel, blocks),
        out_shape=jax.ShapeDtypeStruct((tokens, rows, channels), jnp.bfloat16),
        in_specs=[pl.BlockSpec(memory_space=pltpu.HBM)] * 10,
        out_specs=pl.BlockSpec(memory_space=pltpu.VMEM),
        scratch_shapes=[
            pltpu.VMEM((rows, tokens, channels), jnp.bfloat16),
            pltpu.VMEM((1, tokens), jnp.int32),
            gain,
            pltpu.VMEM((channels, 4 * channels), jnp.bfloat16),
            weight,
            gain,
            weight,
            pltpu.SemaphoreType.DMA((10,)),
            pltpu.VMEM((2, rows, tokens, channels), jnp.bfloat16),
            pltpu.VMEM((rows, tokens, channels), jnp.float32),
            pltpu.VMEM((rows, tokens, channels), jnp.float32),
            pltpu.VMEM((rows, rows, channels), jnp.float32),
            pltpu.VMEM((tokens, channels), jnp.float32),
            pltpu.SemaphoreType.DMA((2, CHUNKS)),
            pltpu.SemaphoreType.DMA((2, CHUNKS)),
            pltpu.SemaphoreType.DMA((CHUNKS // 2,)),
            pltpu.SemaphoreType.DMA((blocks,)),
            pltpu.SemaphoreType.DMA((blocks,)),
        ],
        compiler_params=pltpu.CompilerParams(
            collective_id=0, has_side_effects=True, vmem_limit_bytes=LIMIT
        ),
    )(
        pair,
        residue_mask.reshape(1, tokens),
        ln_in_gain.reshape(1, channels),
        w_a_gate,
        w_a_proj,
        w_b_gate,
        w_b_proj,
        w_out_gate,
        ln_out_gain.reshape(1, channels),
        w_out,
    )


def solution(mesh):
    placed = (P(("groups", "row"), None, None), P("groups"), P(), P(), P(), P(), P(), P(), P(), P())
    return jax.shard_map(
        functools.partial(shards, mesh.shape["row"]),
        mesh=mesh,
        in_specs=placed,
        out_specs=P("groups", "row", None),
        check_vma=False,
    )
```

```python
import functools

import jax
import jax.numpy as jnp
from jax import lax
from jax.experimental import pallas as pl
from jax.experimental.pallas import tpu as pltpu
from jax.sharding import PartitionSpec as P

EPSILON = 1e-05
MESH = pl.DeviceIdType.MESH
CHUNKS = 4
STEPS = 4
GROUP = 1024
LIMIT = 63 * 2**20


def normalize(values, gain):
    center = jnp.mean(values, axis=-1, keepdims=True)
    centered = values - center
    spread = jnp.mean(centered * centered, axis=-1, keepdims=True)
    return centered * lax.rsqrt(spread + EPSILON) * gain


def half_sigmoid(values):
    return 1.0 + jnp.tanh(0.5 * values)


def dot(a, b):
    return jnp.dot(a, b, preferred_element_type=jnp.float32)


def kernel(
    blocks,
    pair,
    mask_arg,
    in_gain_arg,
    w_a_gate,
    w_a_proj,
    w_b_gate,
    w_b_proj,
    w_out_gate_arg,
    out_gain_arg,
    w_out_arg,
    out,
    own_pair,
    mask,
    in_gain,
    w_in,
    w_out_gate,
    out_gain,
    w_out,
    load,
    halo,
    left,
    kept,
    right,
    product,
    token_mask,
    halo_send,
    halo_recv,
    forward_send,
    block_send,
    block_recv,
):
    rows, tokens, channels = pair.shape
    me = lax.axis_index("row")
    odd = lax.rem(me, 2)
    part = rows // CHUNKS
    own = pl.multiple_of(me * rows, rows)

    def at(distance):
        return {"row": lax.rem(me + distance + blocks, blocks)}

    barrier = pltpu.get_barrier_semaphore()

    def greet(distance, _):
        pl.semaphore_signal(barrier, inc=1, device_id=at(distance), device_id_type=MESH)
        return 0

    lax.fori_loop(1, blocks, greet, 0)
    loads = [(pair, own_pair), (mask_arg, mask), (in_gain_arg, in_gain)]
    for n, w in enumerate((w_a_gate, w_a_proj, w_b_gate, w_b_proj)):
        loads.append((w, w_in.at[:, n * channels : (n + 1) * channels]))
    loads += [(w_out_gate_arg, w_out_gate), (out_gain_arg, out_gain), (w_out_arg, w_out)]
    loads = [pltpu.make_async_copy(a, b, load.at[n]) for n, (a, b) in enumerate(loads)]
    for copy in loads:
        copy.start()
    pl.semaphore_wait(barrier, blocks - 1)

    half = CHUNKS // 2

    def span(chunk):
        return pl.ds(chunk * part, part)

    def distance_of(chunk):
        return 1 + odd if chunk >= half else 2

    def direct(chunk):
        distance = distance_of(chunk)
        return pltpu.make_async_remote_copy(
            src_ref=pair.at[span(chunk)],
            dst_ref=halo.at[distance - 1, span(chunk)],
            send_sem=halo_send.at[0, chunk],
            recv_sem=halo_recv.at[distance - 1, chunk],
            device_id=at(-distance),
            device_id_type=MESH,
        )

    def inner(chunk):
        return pltpu.make_async_remote_copy(
            src_ref=pair.at[span(chunk)],
            dst_ref=halo.at[0, span(chunk)],
            send_sem=halo_send.at[1, chunk],
            recv_sem=halo_recv.at[0, chunk],
            device_id=at(-1),
            device_id_type=MESH,
        )

    def halo_all(act):
        for chunk in range(CHUNKS):
            act(direct(chunk))
        for chunk in range(CHUNKS):
            pl.when(odd == 1)(lambda chunk=chunk: act(inner(chunk)))

    halo_all(lambda copy: copy.start())

    def block_copy(distance):
        target = lax.rem(me + distance, blocks)
        columns = pl.ds(pl.multiple_of(target * rows, rows), rows)
        return pltpu.make_async_remote_copy(
            src_ref=pair.at[:, columns],
            dst_ref=out.at[pl.ds(own, rows)],
            send_sem=block_send.at[distance],
            recv_sem=block_recv.at[distance],
            device_id={"row": target},
            device_id_type=MESH,
        )

    def send_block(distance, _):
        block_copy(distance).start()
        return 0

    lax.fori_loop(1, blocks - 2, send_block, 0)

    for copy in loads:
        copy.wait()
    token_mask[...] = jnp.broadcast_to(mask[...].astype(jnp.float32), (channels, tokens)).T

    batch = min(part, max(1, GROUP // tokens))

    def normed_of(values):
        single = jnp.full((channels, channels), 1.0 / channels, jnp.bfloat16)
        double = jnp.full((2 * channels, channels), 1.0 / channels, jnp.bfloat16)
        centered = values.astype(jnp.float32) - dot(values, single)
        square = centered * centered
        high = square.astype(jnp.bfloat16)
        low = (square - high.astype(jnp.float32)).astype(jnp.bfloat16)
        spread = dot(jnp.concatenate([high, low], axis=1), double)
        return (centered * lax.rsqrt(spread + EPSILON) * in_gain[...]).astype(jnp.bfloat16)

    def gated(gates, values):
        return (0.5 * half_sigmoid(gates) * values).reshape(batch, tokens, channels)

    pairs = part * rows

    def work(read, chunk, with_right):
        for n in range(part // batch):
            some = pl.ds(chunk * part + n * batch, batch)
            normed = normed_of(read(some).reshape(batch * tokens, channels))
            a = dot(normed, w_in[:, : 2 * channels])
            values = gated(a[:, :channels], a[:, channels:])
            left[pl.ds(n * batch, batch)] = values.astype(jnp.bfloat16).astype(jnp.float32)
            if with_right:
                b = dot(normed, w_in[:, 2 * channels :])
                values = gated(b[:, :channels], b[:, channels:]) * token_mask[...]
                for i in range(batch):
                    at_row = chunk * part + n * batch + i
                    row = values[i] * token_mask[pl.ds(own + at_row, 1), :]
                    right[at_row] = row.astype(jnp.bfloat16).astype(jnp.float32)

    def combine(read, chunk, owner):
        first = pl.multiple_of(owner * rows, rows) + chunk * part

        def tile(t, _):
            i = (t // (rows // 8)) * 2
            j = pl.multiple_of((t % (rows // 8)) * 8, 8)

            def body(step, sums):
                sums = list(sums)
                for s in range(STEPS):
                    k = pl.ds(pl.multiple_of(step * (8 * STEPS) + s * 8, 8), 8)
                    ls = [left[i + a, k, :] for a in range(2)]
                    for b in range(8):
                        r = right[j + b, k, :]
                        for a in range(2):
                            sums[a * 8 + b] = sums[a * 8 + b] + ls[a] * r
                return tuple(sums)

            zero = jnp.zeros((8, channels), jnp.float32)
            sums = lax.fori_loop(0, tokens // (8 * STEPS), body, (zero,) * 16)
            for a in range(2):
                joined = jnp.concatenate(
                    [jnp.sum(sums[a * 8 + b], axis=0, keepdims=True) for b in range(8)], axis=0
                )
                product[i + a, pl.ds(j, 8), :] = joined * token_mask[pl.ds(first + i + a, 1), :]
            return 0

        lax.fori_loop(0, (part // 2) * (rows // 8), tile, 0)
        normed_x = normalize(product[...], out_gain[...]).astype(jnp.bfloat16)
        update = dot(normed_x.reshape(pairs, channels), w_out[...])
        old = read(pl.ds(chunk * part, part), pl.ds(own, rows))
        normed = normed_of(old.reshape(pairs, channels))
        gating = jax.nn.sigmoid(dot(normed, w_out_gate[...]))
        new = old.astype(jnp.float32) + (gating * update).reshape(part, rows, channels)
        out[pl.ds(first, part)] = new.astype(jnp.bfloat16)

    def own_rows(*index):
        return own_pair[index]

    def own_right(chunk, _):
        work(own_rows, chunk, True)
        kept[pl.ds(chunk * part, part)] = left[...]
        return 0

    lax.fori_loop(0, CHUNKS, own_right, 0)

    def own_chunk(chunk, _):
        left[...] = kept[pl.ds(chunk * part, part)]
        combine(own_rows, chunk, me)
        return 0

    lax.fori_loop(0, CHUNKS, own_chunk, 0)

    def arrival(slot, chunk):
        piece = pl.ds(chunk * part, part)
        return pltpu.make_async_remote_copy(
            src_ref=pair.at[piece],
            dst_ref=halo.at[slot, piece],
            send_sem=halo_send.at[slot, chunk],
            recv_sem=halo_recv.at[slot, chunk],
            device_id=at(1 - 2 * odd),
            device_id_type=MESH,
        )

    def forward(c):
        chunk = odd * half + c
        piece = pl.ds(chunk * part, part)
        return pltpu.make_async_remote_copy(
            src_ref=halo.at[1 - odd, piece],
            dst_ref=halo.at[odd, piece],
            send_sem=forward_send.at[c],
            recv_sem=halo_recv.at[odd, chunk],
            device_id=at(1 - 2 * odd),
            device_id_type=MESH,
        )

    def halo_step(u, _):
        slot = (1 - odd) * (u // 4) + odd * (1 - (u // 2) % 2)
        chunk = (1 - odd) * (u % 4) + odd * (2 * (u // 4) + u % 2)

        @pl.when(u == 4 * odd)
        def _():
            for c in range(half):
                arrival(1 - odd, odd * half + c).wait_recv()
                forward(c).start()

        @pl.when(jnp.logical_or(slot == odd, chunk // half != odd))
        def _():
            arrival(slot, chunk).wait_recv()

        def halo_rows(*index):
            return halo[(slot,) + index]

        work(halo_rows, chunk, False)
        combine(halo_rows, chunk, lax.rem(me + 1 + slot, blocks))
        return 0

    lax.fori_loop(0, 2 * CHUNKS, halo_step, 0)

    for c in range(half):
        forward(c).wait_send()
    halo_all(lambda copy: copy.wait_send())

    def finish_block(distance, _):
        source = lax.rem(me - distance + blocks, blocks)
        columns = pl.ds(own, rows)
        landed = pltpu.make_async_remote_copy(
            src_ref=pair.at[:, columns],
            dst_ref=out.at[pl.ds(pl.multiple_of(source * rows, rows), rows)],
            send_sem=block_send.at[distance],
            recv_sem=block_recv.at[distance],
            device_id={"row": source},
            device_id_type=MESH,
        )
        landed.wait_recv()
        block_copy(distance).wait_send()
        return 0

    lax.fori_loop(1, blocks - 2, finish_block, 0)


def shards(blocks, pair, residue_mask, ln_in_gain, *rest):
    w_a_gate, w_a_proj, w_b_gate, w_b_proj, w_out_gate, ln_out_gain, w_out = rest
    rows, tokens, channels = pair.shape
    weight = pltpu.VMEM((channels, channels), jnp.bfloat16)
    gain = pltpu.VMEM((1, channels), jnp.float32)
    return pl.pallas_call(
        functools.partial(kernel, blocks),
        out_shape=jax.ShapeDtypeStruct((tokens, rows, channels), jnp.bfloat16),
        in_specs=[pl.BlockSpec(memory_space=pltpu.HBM)] * 10,
        out_specs=pl.BlockSpec(memory_space=pltpu.VMEM),
        scratch_shapes=[
            pltpu.VMEM((rows, tokens, channels), jnp.bfloat16),
            pltpu.VMEM((1, tokens), jnp.int32),
            gain,
            pltpu.VMEM((channels, 4 * channels), jnp.bfloat16),
            weight,
            gain,
            weight,
            pltpu.SemaphoreType.DMA((10,)),
            pltpu.VMEM((2, rows, tokens, channels), jnp.bfloat16),
            pltpu.VMEM((rows // CHUNKS, tokens, channels), jnp.float32),
            pltpu.VMEM((rows, tokens, channels), jnp.float32),
            pltpu.VMEM((rows, tokens, channels), jnp.float32),
            pltpu.VMEM((rows // CHUNKS, rows, channels), jnp.float32),
            pltpu.VMEM((tokens, channels), jnp.float32),
            pltpu.SemaphoreType.DMA((2, CHUNKS)),
            pltpu.SemaphoreType.DMA((2, CHUNKS)),
            pltpu.SemaphoreType.DMA((CHUNKS // 2,)),
            pltpu.SemaphoreType.DMA((blocks,)),
            pltpu.SemaphoreType.DMA((blocks,)),
        ],
        compiler_params=pltpu.CompilerParams(
            collective_id=0, has_side_effects=True, vmem_limit_bytes=LIMIT
        ),
    )(
        pair,
        residue_mask.reshape(1, tokens),
        ln_in_gain.reshape(1, channels),
        w_a_gate,
        w_a_proj,
        w_b_gate,
        w_b_proj,
        w_out_gate,
        ln_out_gain.reshape(1, channels),
        w_out,
    )


def solution(mesh):
    placed = (P(("groups", "row"), None, None), P("groups"), P(), P(), P(), P(), P(), P(), P(), P())
    return jax.shard_map(
        functools.partial(shards, mesh.shape["row"]),
        mesh=mesh,
        in_specs=placed,
        out_specs=P("groups", "row", None),
        check_vma=False,
    )
```

```python
import functools

import jax
import jax.numpy as jnp
from jax import lax
from jax.experimental import pallas as pl
from jax.experimental.pallas import tpu as pltpu
from jax.sharding import PartitionSpec as P

EPSILON = 1e-05
MESH = pl.DeviceIdType.MESH
CHUNKS = 4
STEPS = 8
GROUP = 1024
FIRST = 1
LIMIT = 63 * 2**20


def normalize(values, gain):
    center = jnp.mean(values, axis=-1, keepdims=True)
    centered = values - center
    spread = jnp.mean(centered * centered, axis=-1, keepdims=True)
    return centered * lax.rsqrt(spread + EPSILON) * gain


def half_sigmoid(values):
    return 1.0 + jnp.tanh(0.5 * values)


def dot(a, b):
    return jnp.dot(a, b, preferred_element_type=jnp.float32)


def kernel(
    blocks,
    pair,
    mask_arg,
    in_gain_arg,
    w_a_gate,
    w_a_proj,
    w_b_gate,
    w_b_proj,
    w_out_gate_arg,
    out_gain_arg,
    w_out_arg,
    out,
    own_pair,
    mask,
    in_gain,
    w_in,
    w_out_gate,
    out_gain,
    w_out,
    load,
    halo,
    relay,
    left,
    kept,
    right,
    product,
    token_mask,
    halo_send,
    halo_recv,
    forward_send,
    block_send,
    block_recv,
    relay_send,
    relay_recv,
):
    rows, tokens, channels = pair.shape
    me = lax.axis_index("row")
    odd = lax.rem(me, 2)
    part = rows // CHUNKS
    own = pl.multiple_of(me * rows, rows)

    def at(distance):
        return {"row": lax.rem(me + distance + blocks, blocks)}

    barrier = pltpu.get_barrier_semaphore()

    def greet(distance, _):
        pl.semaphore_signal(barrier, inc=1, device_id=at(distance), device_id_type=MESH)
        return 0

    lax.fori_loop(1, blocks, greet, 0)
    loads = [(pair, own_pair), (mask_arg, mask), (in_gain_arg, in_gain)]
    for n, w in enumerate((w_a_gate, w_a_proj, w_b_gate, w_b_proj)):
        loads.append((w, w_in.at[:, n * channels : (n + 1) * channels]))
    loads += [(w_out_gate_arg, w_out_gate), (out_gain_arg, out_gain), (w_out_arg, w_out)]
    loads = [pltpu.make_async_copy(a, b, load.at[n]) for n, (a, b) in enumerate(loads)]
    for copy in loads:
        copy.start()
    pl.semaphore_wait(barrier, blocks - 1)

    half = CHUNKS // 2

    def span(chunk):
        return pl.ds(chunk * part, part)

    def distance_of(chunk):
        return 1 + odd if chunk >= half else 2

    def direct(chunk):
        distance = distance_of(chunk)
        return pltpu.make_async_remote_copy(
            src_ref=pair.at[span(chunk)],
            dst_ref=halo.at[distance - 1, span(chunk)],
            send_sem=halo_send.at[0, chunk],
            recv_sem=halo_recv.at[distance - 1, chunk],
            device_id=at(-distance),
            device_id_type=MESH,
        )

    def inner(chunk):
        return pltpu.make_async_remote_copy(
            src_ref=pair.at[span(chunk)],
            dst_ref=halo.at[0, span(chunk)],
            send_sem=halo_send.at[1, chunk],
            recv_sem=halo_recv.at[0, chunk],
            device_id=at(-1),
            device_id_type=MESH,
        )

    def halo_all(act):
        for chunk in range(CHUNKS):
            act(direct(chunk))
        for chunk in range(CHUNKS):
            pl.when(odd == 1)(lambda chunk=chunk: act(inner(chunk)))

    halo_all(lambda copy: copy.start())

    def block_copy(distance):
        target = lax.rem(me + distance, blocks)
        columns = pl.ds(pl.multiple_of(target * rows, rows), rows)
        return pltpu.make_async_remote_copy(
            src_ref=pair.at[:, columns],
            dst_ref=out.at[pl.ds(own, rows)],
            send_sem=block_send.at[distance],
            recv_sem=block_recv.at[distance],
            device_id={"row": target},
            device_id_type=MESH,
        )

    def relayed(source, distance):
        chip = source // 2
        target_chip = lax.rem(source + distance, blocks) // 2
        across = jnp.logical_and(lax.rem(chip, 2) == 0, lax.rem(target_chip, 2) == 1)
        return jnp.logical_and(across, target_chip != chip + 1)

    def to_relay(distance, source, device):
        target = lax.rem(source + distance, blocks)
        columns = pl.ds(pl.multiple_of(target * rows, rows), rows)
        return pltpu.make_async_remote_copy(
            src_ref=pair.at[:, columns],
            dst_ref=relay.at[distance],
            send_sem=block_send.at[distance],
            recv_sem=relay_recv.at[distance],
            device_id={"row": device},
            device_id_type=MESH,
        )

    before = lax.rem(me + blocks - 2, blocks)
    after = lax.rem(me + 2, blocks)

    def from_relay(distance):
        return pltpu.make_async_remote_copy(
            src_ref=relay.at[distance],
            dst_ref=out.at[pl.ds(pl.multiple_of(before * rows, rows), rows)],
            send_sem=relay_send.at[distance],
            recv_sem=block_recv.at[distance],
            device_id={"row": lax.rem(before + distance, blocks)},
            device_id_type=MESH,
        )

    def send_relayed(distance, _):
        @pl.when(relayed(me, distance))
        def _():
            to_relay(distance, me, after).start()

        return 0

    def send_block(distance, _):
        @pl.when(jnp.logical_not(relayed(me, distance)))
        def _():
            block_copy(distance).start()

        return 0

    lax.fori_loop(1, blocks - 2, send_relayed, 0)
    lax.fori_loop(1, blocks - 2, send_block, 0)

    def pass_on(distance, _):
        @pl.when(relayed(before, distance))
        def _():
            to_relay(distance, before, before).wait_recv()
            from_relay(distance).start()

        return 0

    share = -(-(blocks - 3) // (2 * CHUNKS - FIRST))

    for copy in loads:
        copy.wait()
    token_mask[...] = jnp.broadcast_to(mask[...].astype(jnp.float32), (channels, tokens)).T

    batch = min(part, max(1, GROUP // tokens))

    def normed_of(values):
        single = jnp.full((channels, channels), 1.0 / channels, jnp.bfloat16)
        double = jnp.full((2 * channels, channels), 1.0 / channels, jnp.bfloat16)
        centered = values.astype(jnp.float32) - dot(values, single)
        square = centered * centered
        high = square.astype(jnp.bfloat16)
        low = (square - high.astype(jnp.float32)).astype(jnp.bfloat16)
        spread = dot(jnp.concatenate([high, low], axis=1), double)
        return (centered * lax.rsqrt(spread + EPSILON) * in_gain[...]).astype(jnp.bfloat16)

    def gated(gates, values):
        return (0.5 * half_sigmoid(gates) * values).reshape(batch, tokens, channels)

    pairs = part * rows

    def work(read, chunk, with_right):
        for n in range(part // batch):
            some = pl.ds(chunk * part + n * batch, batch)
            normed = normed_of(read(some).reshape(batch * tokens, channels))
            a = dot(normed, w_in[:, : 2 * channels])
            values = gated(a[:, :channels], a[:, channels:])
            left[pl.ds(n * batch, batch)] = values.astype(jnp.bfloat16).astype(jnp.float32)
            if with_right:
                b = dot(normed, w_in[:, 2 * channels :])
                values = gated(b[:, :channels], b[:, channels:]) * token_mask[...]
                for i in range(batch):
                    at_row = chunk * part + n * batch + i
                    row = values[i] * token_mask[pl.ds(own + at_row, 1), :]
                    right[at_row] = row.astype(jnp.bfloat16).astype(jnp.float32)

    def combine(read, chunk, owner):
        first = pl.multiple_of(owner * rows, rows) + chunk * part

        def tile(t, _):
            i = (t // (rows // 8)) * 2
            j = pl.multiple_of((t % (rows // 8)) * 8, 8)

            def body(step, sums):
                sums = list(sums)
                for s in range(STEPS):
                    k = pl.ds(pl.multiple_of(step * (8 * STEPS) + s * 8, 8), 8)
                    ls = [left[i + a, k, :] for a in range(2)]
                    for b in range(8):
                        r = right[j + b, k, :]
                        for a in range(2):
                            sums[a * 8 + b] = sums[a * 8 + b] + ls[a] * r
                return tuple(sums)

            zero = jnp.zeros((8, channels), jnp.float32)
            sums = lax.fori_loop(0, tokens // (8 * STEPS), body, (zero,) * 16)
            for a in range(2):
                joined = jnp.concatenate(
                    [jnp.sum(sums[a * 8 + b], axis=0, keepdims=True) for b in range(8)], axis=0
                )
                product[i + a, pl.ds(j, 8), :] = joined * token_mask[pl.ds(first + i + a, 1), :]
            return 0

        lax.fori_loop(0, (part // 2) * (rows // 8), tile, 0)
        normed_x = normalize(product[...], out_gain[...]).astype(jnp.bfloat16)
        update = dot(normed_x.reshape(pairs, channels), w_out[...])
        old = read(pl.ds(chunk * part, part), pl.ds(own, rows))
        normed = normed_of(old.reshape(pairs, channels))
        gating = jax.nn.sigmoid(dot(normed, w_out_gate[...]))
        new = old.astype(jnp.float32) + (gating * update).reshape(part, rows, channels)
        out[pl.ds(first, part)] = new.astype(jnp.bfloat16)

    def own_rows(*index):
        return own_pair[index]

    def own_right(chunk, _):
        work(own_rows, chunk, True)
        kept[pl.ds(chunk * part, part)] = left[...]
        return 0

    lax.fori_loop(0, CHUNKS, own_right, 0)

    def own_chunk(chunk, _):
        left[...] = kept[pl.ds(chunk * part, part)]
        combine(own_rows, chunk, me)
        return 0

    lax.fori_loop(0, CHUNKS, own_chunk, 0)

    def arrival(slot, chunk):
        piece = pl.ds(chunk * part, part)
        return pltpu.make_async_remote_copy(
            src_ref=pair.at[piece],
            dst_ref=halo.at[slot, piece],
            send_sem=halo_send.at[slot, chunk],
            recv_sem=halo_recv.at[slot, chunk],
            device_id=at(1 - 2 * odd),
            device_id_type=MESH,
        )

    def forward(c):
        chunk = odd * half + c
        piece = pl.ds(chunk * part, part)
        return pltpu.make_async_remote_copy(
            src_ref=halo.at[1 - odd, piece],
            dst_ref=halo.at[odd, piece],
            send_sem=forward_send.at[c],
            recv_sem=halo_recv.at[odd, chunk],
            device_id=at(1 - 2 * odd),
            device_id_type=MESH,
        )

    def halo_step(u, _):
        slot = (1 - odd) * (u // 4) + odd * (1 - (u // 2) % 2)
        chunk = (1 - odd) * (u % 4) + odd * (2 * (u // 4) + u % 2)

        @pl.when(u == 4 * odd)
        def _():
            for c in range(half):
                arrival(1 - odd, odd * half + c).wait_recv()
                forward(c).start()

        @pl.when(jnp.logical_or(slot == odd, chunk // half != odd))
        def _():
            arrival(slot, chunk).wait_recv()

        lower = jnp.minimum(1 + jnp.maximum(u - FIRST, 0) * share, blocks - 2)
        upper = jnp.minimum(1 + jnp.maximum(u + 1 - FIRST, 0) * share, blocks - 2)
        lax.fori_loop(lower, upper, pass_on, 0)

        def halo_rows(*index):
            return halo[(slot,) + index]

        work(halo_rows, chunk, False)
        combine(halo_rows, chunk, lax.rem(me + 1 + slot, blocks))
        return 0

    lax.fori_loop(0, 2 * CHUNKS, halo_step, 0)

    for c in range(half):
        forward(c).wait_send()
    halo_all(lambda copy: copy.wait_send())

    def finish_block(distance, _):
        source = lax.rem(me - distance + blocks, blocks)
        columns = pl.ds(own, rows)
        landed = pltpu.make_async_remote_copy(
            src_ref=pair.at[:, columns],
            dst_ref=out.at[pl.ds(pl.multiple_of(source * rows, rows), rows)],
            send_sem=block_send.at[distance],
            recv_sem=block_recv.at[distance],
            device_id={"row": source},
            device_id_type=MESH,
        )
        landed.wait_recv()
        block_copy(distance).wait_send()

        @pl.when(relayed(before, distance))
        def _():
            from_relay(distance).wait_send()

        return 0

    lax.fori_loop(1, blocks - 2, finish_block, 0)


def shards(blocks, pair, residue_mask, ln_in_gain, *rest):
    w_a_gate, w_a_proj, w_b_gate, w_b_proj, w_out_gate, ln_out_gain, w_out = rest
    rows, tokens, channels = pair.shape
    weight = pltpu.VMEM((channels, channels), jnp.bfloat16)
    gain = pltpu.VMEM((1, channels), jnp.float32)
    return pl.pallas_call(
        functools.partial(kernel, blocks),
        out_shape=jax.ShapeDtypeStruct((tokens, rows, channels), jnp.bfloat16),
        in_specs=[pl.BlockSpec(memory_space=pltpu.HBM)] * 10,
        out_specs=pl.BlockSpec(memory_space=pltpu.VMEM),
        scratch_shapes=[
            pltpu.VMEM((rows, tokens, channels), jnp.bfloat16),
            pltpu.VMEM((1, tokens), jnp.int32),
            gain,
            pltpu.VMEM((channels, 4 * channels), jnp.bfloat16),
            weight,
            gain,
            weight,
            pltpu.SemaphoreType.DMA((10,)),
            pltpu.VMEM((2, rows, tokens, channels), jnp.bfloat16),
            pltpu.VMEM((blocks, rows, rows, channels), jnp.bfloat16),
            pltpu.VMEM((rows // CHUNKS, tokens, channels), jnp.float32),
            pltpu.VMEM((rows, tokens, channels), jnp.float32),
            pltpu.VMEM((rows, tokens, channels), jnp.float32),
            pltpu.VMEM((rows // CHUNKS, rows, channels), jnp.float32),
            pltpu.VMEM((tokens, channels), jnp.float32),
            pltpu.SemaphoreType.DMA((2, CHUNKS)),
            pltpu.SemaphoreType.DMA((2, CHUNKS)),
            pltpu.SemaphoreType.DMA((CHUNKS // 2,)),
            pltpu.SemaphoreType.DMA((blocks,)),
            pltpu.SemaphoreType.DMA((blocks,)),
            pltpu.SemaphoreType.DMA((blocks,)),
            pltpu.SemaphoreType.DMA((blocks,)),
        ],
        compiler_params=pltpu.CompilerParams(
            collective_id=0, has_side_effects=True, vmem_limit_bytes=LIMIT
        ),
    )(
        pair,
        residue_mask.reshape(1, tokens),
        ln_in_gain.reshape(1, channels),
        w_a_gate,
        w_a_proj,
        w_b_gate,
        w_b_proj,
        w_out_gate,
        ln_out_gain.reshape(1, channels),
        w_out,
    )


def solution(mesh):
    placed = (P(("groups", "row"), None, None), P("groups"), P(), P(), P(), P(), P(), P(), P(), P())
    return jax.shard_map(
        functools.partial(shards, mesh.shape["row"]),
        mesh=mesh,
        in_specs=placed,
        out_specs=P("groups", "row", None),
        check_vma=False,
    )
```
